512 devices in a mesh: gx: 16 (over y, z_lo), gy: 4 (over z_hi), gz: 8 (over x, core).
Axes of the slice: x: 4, y: 4, z: 16 (z_hi: 4, z_lo: 4; z = z_hi * 4 + z_lo), core: 2. Of those that a mesh axis runs over, the one named last changes fastest.
Arguments:
- ref_image: bfloat16 [4096, 64, 1024], P('gx', 'gy', 'gz'), may hold values from -6 to 6
- def_image: bfloat16 [4096, 64, 1024], P('gx', 'gy', 'gz'), may hold values from -6 to 6
- displacement: float32 [3, 512, 8, 128], P(None, 'gx', 'gy', 'gz'), may hold values from -3 to 3
Outputs:
- new_displacement: float32 [3, 512, 8, 128], P(None, 'gx', 'gy', 'gz')
- fine_residual: bfloat16 [4096, 64, 1024], P('gx', 'gy', 'gz')
The draws below stay inside these ranges and needn't reach their ends.
All inputs are finite; a program needn't handle non-finite values.
Results may differ from the reference program's by a relative error of at most 0.0022.
Values may be sent and summed in bfloat16 or wider, within the bound.
No kernel may reach another device: no remote copies, remote signals or barrier semaphores. Data moves between devices by JAX's collectives and lax.ppermute only.
A program may use at most 64 MiB of HBM per device.

```python
import jax
import jax.numpy as jnp
from jax import lax

NX = 4096
NY = 64
NZ = 1024
MX = 512
MY = 8
MZ = 128


def steps_of(stream_key, dims, pieces, low, high):
    def one(position, parts):
        draws = jax.random.uniform(jax.random.fold_in(jax.random.fold_in(stream_key, 6), position), (parts,), jnp.float32, low / len(pieces), high / len(pieces))
        return jnp.repeat(jnp.exp(draws), dims[position] // parts).reshape((-1,) + (1,) * (len(dims) - position - 1))

    factor_of = one(*pieces[0])
    for cut in pieces[1:]:
        factor_of = factor_of * one(*cut)
    return factor_of


def noise(rng, extent, width, most, pieces=(), kind=jnp.bfloat16):
    values = jax.random.normal(rng, extent, jnp.float32) * width
    if len(pieces) > 0:
        values = steps_of(rng, extent, pieces, -0.22, 0.18) * values
    return jnp.clip(values, min=-most, max=most).astype(kind)


def setup_inputs(seed: int = 0) -> dict:
    key_list = jax.random.split(jax.random.key(seed), 4)
    return {
        "ref_image": noise(key_list[0], (NX, NY, NZ), 1.0, 6.0, ((0, 16), (1, 4), (2, 8))),
        "def_image": noise(key_list[1], (NX, NY, NZ), 1.0, 6.0, ((0, 16), (1, 4), (2, 8))),
        "displacement": noise(key_list[2], (3, MX, MY, MZ), 0.5, 3.0, ((1, 16), (2, 4), (3, 8)), jnp.float32),
    }


stiffness = 64.0

def bin_level(image):
    values = image.astype(jnp.float32)
    sizex, sizey, sizez = values.shape
    return values.reshape(sizex // 8, 8, sizey // 8, 8, sizez // 8, 8).sum((1, 3, 5)) / 32.0

def central(padded):
    slope_x = (padded[2:, 1:-1, 1:-1] - padded[:-2, 1:-1, 1:-1]) / 2.0
    slope_y = (padded[1:-1, 2:, 1:-1] - padded[1:-1, :-2, 1:-1]) / 2.0
    slope_z = (padded[1:-1, 1:-1, 2:] - padded[1:-1, 1:-1, :-2]) / 2.0
    return (slope_x, slope_y, slope_z)

def line_matrix(count):
    return jnp.eye(count, dtype=jnp.float32) * (1.0 + 2.0 * stiffness) - stiffness * (jnp.eye(count, k=1, dtype=jnp.float32) + jnp.eye(count, k=-1, dtype=jnp.float32))

def prolong_table(fine_count, coarse_count):
    index = jnp.arange(fine_count)
    center = index // 8 + 1
    offset = ((index % 8).astype(jnp.float32) + 0.5) / 8.0 - 0.5
    column = jnp.arange(coarse_count + 2)[None, :]
    weight = jnp.where(column == center[:, None], 1.0 - jnp.abs(offset)[:, None], 0.0)
    weight = weight + jnp.where((offset[:, None] >= 0.0) & (column == center[:, None] + 1), offset[:, None], 0.0)
    weight = weight + jnp.where((offset[:, None] < 0.0) & (column == center[:, None] - 1), -offset[:, None], 0.0)
    return weight.astype(jnp.float32)

def reference(ref_image, def_image, displacement):
    coarse_ref = bin_level(ref_image)
    coarse_def = bin_level(def_image)
    slopes = central(jnp.pad(coarse_ref, 1))
    mismatch = coarse_def - coarse_ref - (slopes[0] * displacement[0] + slopes[1] * displacement[1] + slopes[2] * displacement[2])
    rhs = jnp.stack([slope * mismatch for slope in slopes])
    lines = rhs.shape[1]
    factor = jnp.linalg.cholesky(line_matrix(lines))
    flat = jnp.moveaxis(rhs, 1, 0).reshape(lines, -1)
    solved = jax.scipy.linalg.cho_solve((factor, True), flat)
    step = jnp.moveaxis(solved.reshape(lines, 3, rhs.shape[2], rhs.shape[3]), 0, 1)
    new_displacement = displacement + step
    padded = jnp.pad(new_displacement, ((0, 0), (1, 1), (1, 1), (1, 1)))
    table_x = prolong_table(ref_image.shape[0], rhs.shape[1])
    table_y = prolong_table(ref_image.shape[1], rhs.shape[2])
    table_z = prolong_table(ref_image.shape[2], rhs.shape[3])
    grads = central(jnp.pad(ref_image.astype(jnp.float32), 1))
    total = def_image.astype(jnp.float32) - ref_image.astype(jnp.float32)
    for component in range(3):
        field = jnp.einsum('ia,abc->ibc', table_x, padded[component], precision=lax.Precision.HIGHEST)
        field = jnp.einsum('jb,ibc->ijc', table_y, field, precision=lax.Precision.HIGHEST)
        field = jnp.einsum('ijc,kc->ijk', field, table_z, precision=lax.Precision.HIGHEST)
        total = total - grads[component] * field
    return (new_displacement, total.astype(jnp.bfloat16))
```

```python
import numpy as np
import jax
import jax.numpy as jnp
from jax import lax
from jax.experimental import pallas as pl
from jax.experimental.pallas import tpu as pltpu
from jax.sharding import PartitionSpec as P

STIFFNESS = 64.0
SPAN = 20
VMEM = pl.BlockSpec(memory_space=pltpu.VMEM)
HIGHEST = lax.Precision.HIGHEST
F32 = jnp.float32
BF16 = jnp.bfloat16
SLAB = 40
EXT = 40


def inverse_entry(lines):
    diagonal = 1.0 + 2.0 * STIFFNESS
    root = (diagonal - np.sqrt(diagonal**2 - 4.0 * STIFFNESS**2)) / (2.0 * STIFFNESS)
    theta = -np.log(root)
    scale = 1.0 / (2.0 * STIFFNESS * np.sinh(theta) * (1.0 - root ** (2.0 * (lines + 1))))

    def first(i):
        return 1.0 - root ** (2.0 * (i + 1))

    def last(i):
        return 1.0 - root ** (2.0 * (lines - i))

    return root, scale, first, last


def solve_tables(devices, cells):
    lines = devices * cells
    root, scale, first, last = inverse_entry(lines)
    local = np.arange(cells)
    weights = np.zeros((devices, 8, cells))
    table = np.zeros((devices, EXT, cells + 4 * devices))
    everyone = np.arange(devices)
    for p in range(devices):
        at = p * cells + local
        weights[p, 0] = first(at) * root ** (cells - 1.0 - local)
        weights[p, 1] = last(at) * root**local
        rows = np.concatenate([at, [p * cells - 1, p * cells + cells]])[:, None]
        used = slice(0, cells + 2)

        def entry(columns):
            low, high = np.minimum(rows, columns), np.maximum(rows, columns)
            return scale * root ** (1.0 * (high - low)) * first(low) * last(high)

        table[p, used, :cells] = entry(at[None, :])
        below = (everyone < p)[None, :]
        gap = np.where(below, rows - (everyone * cells + cells - 1)[None, :], 0)
        table[p, used, cells : cells + devices] = below * scale * last(rows) * root ** (1.0 * gap)
        above = (everyone > p)[None, :]
        gap = np.where(above, (everyone * cells)[None, :] - rows, 0)
        table[p, used, cells + devices : cells + 2 * devices] = (
            above * scale * first(rows) * root ** (1.0 * gap)
        )
        table[p, used, cells + 2 * devices : cells + 3 * devices] = entry(
            (everyone * cells)[None, :]
        )
        table[p, used, cells + 3 * devices :] = entry((everyone * cells + cells - 1)[None, :])
    return weights.astype(np.float32), table.astype(np.float32)


def iota(shape, dim):
    return lax.broadcasted_iota(jnp.int32, shape, dim)


def roll(value, shift, axis):
    size = value.shape[axis]
    return pltpu.roll(value, shift % size, axis)


def exact_dot(a, b, dims):
    return lax.dot_general(a, b, (dims, ((), ())), precision=HIGHEST, preferred_element_type=F32)


def put_split(ref, start, value):
    rows = value.shape[0]
    for part in range(3):
        piece = value.astype(BF16)
        ref[pl.ds(start + part * rows, rows), :] = piece
        value = value - piece.astype(F32)


def get_split(ref, rows):
    return (
        ref[0:rows, :].astype(F32)
        + ref[rows : 2 * rows, :].astype(F32)
        + ref[2 * rows : 3 * rows, :].astype(F32)
    )


def bin_kernel(
    chunk, ref_ref, def_ref, disp_ref,
    coarse_ref, up_ref, down_ref, y_high_ref, y_low_ref,
    bins, faces,
):
    step = pl.program_id(0)
    cells = chunk // 8
    row0 = pl.multiple_of(step * cells, cells)
    for k, image in enumerate((ref_ref, def_ref)):
        for c in range(cells):
            planes = image[pl.ds(c * 8, 8)].astype(F32)
            total = planes.sum(0)
            for y in range(2):
                bins[k, y, pl.ds(row0 + c, 1), :] = total[y * 8 : y * 8 + 8].sum(
                    0, keepdims=True
                )
    flat = ref_ref[...].reshape(chunk * 16, 128)
    lane = iota((16, 128), 1)
    row = iota((16, 128), 0)
    pick = jnp.where(
        ((row == 0) & (lane == 127)) | ((row == 1) & (lane == 0)), 1.0, 0.0
    ).astype(BF16)
    sides = lax.dot_general(
        pick, flat, (((1,), (1,)), ((), ())), preferred_element_type=F32
    )
    for c in range(cells):
        faces[0, pl.ds(row0 + c, 1), :] = sides[0:1, c * 128 : (c + 1) * 128]
        faces[1, pl.ds(row0 + c, 1), :] = sides[1:2, c * 128 : (c + 1) * 128]
    wide = ref_ref[...].astype(F32)
    x0 = pl.multiple_of(step * chunk, chunk)
    y_high_ref[pl.ds(x0, chunk), :] = wide[:, 15, :].astype(BF16)
    y_low_ref[pl.ds(x0, chunk), :] = wide[:, 0, :].astype(BF16)

    @pl.when(step == pl.num_programs(0) - 1)
    def _():
        rows = bins.shape[2]
        z = iota((128, 128), 0) // 8
        lanes = iota((128, 128), 1)
        place_lanes = iota((16, 128), 1)
        place_z = iota((16, 128), 0)
        whole = []
        for y in range(2):
            total = jnp.zeros((rows, 128), F32)
            for k in range(2):
                summer = jnp.where(lanes == k * SPAN + 2 + z, 1.0 / 32.0, 0.0)
                total += exact_dot(bins[k, y], summer, ((1,), (0,)))
            for k in range(3):
                place = jnp.where(place_lanes == (2 + k) * SPAN + 2 + place_z, 1.0, 0.0)
                total += exact_dot(disp_ref[k, y], place, ((0,), (0,)))
            coarse_ref[y] = total
            whole.append(total)
        position = iota((rows, 128), 1) % SPAN
        up = jnp.where(position < 2, roll(whole[0], -16, 1), roll(whole[1], -12, 1))
        down = jnp.where(position >= 18, roll(whole[0], 16, 1), roll(whole[1], 12, 1))
        put_split(up_ref, 0, up)
        put_split(down_ref, 0, down)
        up_ref[pl.ds(3 * rows, 32), :] = faces[0].astype(BF16)
        down_ref[pl.ds(3 * rows, 32), :] = faces[1].astype(BF16)


def z_kernel(
    devices, coarse_in, low_in, high_in, y_high_in, y_low_in, coarse_out, first_out, second_out
):
    rows = coarse_in.shape[1]
    me = lax.axis_index("gz")
    lane = iota((rows, 128), 1)
    position = lane % SPAN
    inside = lane < 5 * SPAN
    low = jnp.where(me > 0, get_split(low_in, rows), 0.0)
    high = jnp.where(me < devices - 1, get_split(high_in, rows), 0.0)
    whole = []
    for y in range(2):
        value = coarse_in[y]
        value = jnp.where((position < 2) & inside, roll(low, -4 * y, 1), value)
        value = jnp.where((position >= 18) & inside, roll(high, 4 * y, 1), value)
        coarse_out[y] = value
        whole.append(value)
    up = jnp.where(inside, whole[1], roll(whole[0], 100, 1))
    down = jnp.where(inside, whole[0], roll(whole[1], 100, 1))
    even = me % 2 == 0
    put_split(first_out, 0, jnp.where(even, up, down))
    put_split(second_out, 0, jnp.where(even, down, up))
    fine = y_high_in.shape[0]
    high_face, low_face = y_high_in[...], y_low_in[...]
    first_out[pl.ds(3 * rows, fine), :] = jnp.where(even, high_face, low_face)
    second_out[pl.ds(3 * rows, fine), :] = jnp.where(even, low_face, high_face)


def rhs_kernel(
    coarse_in, first_in, second_in, plane_low, plane_high, weights_in,
    slab_out, rhs_out, disp_out,
):
    rows = coarse_in.shape[1]
    devices = slab_out.shape[0]
    me = lax.axis_index("gx")
    even = lax.axis_index("gz") % 2 == 0
    first, second = get_split(first_in, rows), get_split(second_in, rows)
    below = jnp.where(even, first, second)
    above = jnp.where(even, second, first)
    layers = [below, coarse_in[0], coarse_in[1], above]
    lane = iota((rows, 128), 1)
    group = lane // 32
    position = lane % 32
    row = iota((rows, 128), 0)

    def packed(sources):
        value = jnp.zeros((rows, 128), F32)
        for y, (layer, at) in enumerate(sources):
            value = jnp.where(group == y, roll(layer, 32 * y - at, 1), value)
        return jnp.where(position < SPAN, value, 0.0)

    cell = packed([(layer, 0) for layer in layers])
    cell_below = packed([(below, 100), (layers[0], 0), (layers[1], 0), (layers[2], 0)])
    cell_above = packed([(layers[1], 0), (layers[2], 0), (layers[3], 0), (above, 100)])
    cell_def = packed([(layer, SPAN) for layer in layers])
    disp = [packed([(layer, (2 + k) * SPAN) for layer in layers]) for k in range(3)]
    slope_y = (cell_above - cell_below) * 0.5
    slope_z = (roll(cell, -1, 1) - roll(cell, 1, 1)) * 0.5
    slope_x = (roll(cell, -1, 0) - roll(cell, 1, 0)) * 0.5
    partial = cell_def - cell - (slope_y * disp[1] + slope_z * disp[2])
    mismatch = partial - slope_x * disp[0]
    keep = (position >= 1) & (position < SPAN - 1) & (row > 0) & (row < rows - 1)
    weights = weights_in[me]
    lines = []
    sums = []
    for k, slope in enumerate((slope_x, slope_y, slope_z)):
        rhs = jnp.where(keep, slope * mismatch, 0.0)
        rhs_out[k] = rhs
        disp_out[k] = disp[k]
        sums.append(exact_dot(weights, rhs, ((1,), (0,))))
    lines += [s[0:1] for s in sums] + [s[1:2] for s in sums]
    end = rows - 1
    lines += [cell[i : i + 1] for i in (0, 1, end - 1, end)]
    for value in (partial, slope_y, slope_z, disp[0]):
        lines += [value[0:1], value[end:]]
    lines += [disp[1][0:1], disp[2][0:1], disp[1][end:], disp[2][end:]]
    for i, line in enumerate(lines):
        for q in range(devices):
            slab_out[q, i : i + 1, :] = line
    low_plane = plane_low[0].astype(F32)
    high_plane = plane_high[0].astype(F32)
    blank = jnp.zeros((24 - len(lines), 128), F32)
    for q in range(devices):
        slab_out[q, len(lines) : 24, :] = blank
        slab_out[q, 24:40, :] = jnp.where(me > q, low_plane, high_plane)


def fine_kernel(
    chunk, slab_in, rhs_in, disp_in, table_in, z_low_in, z_high_in, first_in, second_in,
    ref_ref, before_ref, after_ref, def_ref,
    disp_out, out_ref,
    field, z_faces, y_faces,
):
    step = pl.program_id(0)
    devices = slab_in.shape[0]
    rows = rhs_in.shape[1]
    me = lax.axis_index("gx")
    me_z = lax.axis_index("gz")
    last_z = lax.axis_size("gz") - 1
    even = me_z % 2 == 0
    lower = jnp.maximum(me - 1, 0)
    upper = jnp.minimum(me + 1, devices - 1)

    @pl.when(step == 0)
    def _():
        lane = iota((devices, 128), 1)
        position = lane % 32
        q = iota((devices, 128), 0)
        keep = (position >= 1) & (position < SPAN - 1)

        def line(i):
            return slab_in[:, i, :]

        from_below = jnp.where(q > 0, roll(line(9), 1, 0), 0.0)
        from_above = jnp.where(q < devices - 1, roll(line(6), -1, 0), 0.0)
        slopes_0 = ((line(7) - from_below) * 0.5, line(12), line(14))
        slopes_1 = ((from_above - line(8)) * 0.5, line(13), line(15))
        mismatch_0 = line(10) - slopes_0[0] * line(16)
        mismatch_1 = line(11) - slopes_1[0] * line(17)
        own_lane = iota((16, 128), 1)
        own_z = iota((16, 128), 0)
        edge = iota((8, 128), 0)
        edge_lane = iota((8, 128), 1) % 32
        edge_keep = (edge_lane >= 1) & (edge_lane < SPAN - 1)
        solved = []
        for k in range(3):
            edge_0 = jnp.where(keep, slopes_0[k] * mismatch_0, 0.0)
            edge_1 = jnp.where(keep, slopes_1[k] * mismatch_1, 0.0)
            known = jnp.concatenate([rhs_in[k], line(k), line(3 + k), edge_0, edge_1], axis=0)
            moved = exact_dot(table_in[me], known, ((1,), (0,)))
            low_row = slab_in[lower, 17 if k == 0 else 19 + k : (17 if k == 0 else 19 + k) + 1, :]
            high_row = slab_in[upper, 16 if k == 0 else 17 + k : (16 if k == 0 else 17 + k) + 1, :]
            low_row = jnp.where(me > 0, low_row, 0.0)
            high_row = jnp.where(me < devices - 1, high_row, 0.0)
            outer = jnp.where(edge == 0, low_row, jnp.where(edge == 1, high_row, 0.0))
            inner = moved[:rows] + disp_in[k]
            outer = jnp.where(edge_keep, outer + moved[rows:], 0.0)
            for y in range(2):
                pick = jnp.where(own_lane == 32 * (y + 1) + 2 + own_z, 1.0, 0.0)
                disp_out[k, y] = exact_dot(pick, inner, ((1,), (1,)))
            inner_lane = iota((rows, 128), 1) % 32
            inner = jnp.where((inner_lane >= 1) & (inner_lane < SPAN - 1), inner, 0.0)
            solved += [inner, outer]
        whole = jnp.concatenate(solved, axis=0)
        parts = []
        for _ in range(3):
            piece = whole.astype(BF16)
            parts.append(piece)
            whole = whole - piece.astype(F32)
        height = 3 * EXT
        stack = jnp.concatenate(parts, axis=0)
        z_faces[0] = jnp.where(me_z > 0, z_low_in[...].astype(F32), 0.0)
        z_faces[1] = jnp.where(me_z < last_z, z_high_in[...].astype(F32), 0.0)
        y_first, y_second = first_in[...].astype(F32), second_in[...].astype(F32)
        y_faces[0] = jnp.where(even, y_first, y_second)
        y_faces[1] = jnp.where(even, y_second, y_first)
        source = iota((128, 128), 0)
        fine_z = iota((128, 128), 1).astype(F32)
        coarse_z = (source % 32 - 2).astype(F32)
        coarse_y = (source // 32 - 1).astype(F32)
        along_z = jnp.maximum(
            1.0 - jnp.abs(fine_z * 0.125 + (0.0625 - 0.5) - coarse_z), 0.0
        )
        for y in range(16):
            at = (y + 0.5) / 8.0 - 0.5
            along_y = jnp.maximum(0.5 - 0.5 * jnp.abs(at - coarse_y), 0.0)
            product = jnp.dot(
                stack, (along_z * along_y).astype(BF16), preferred_element_type=F32
            )
            field[pl.ds(y * height, height), :] = (
                product[:height] + product[height : 2 * height] + product[2 * height :]
            )

    height = 3 * EXT
    cells = chunk // 8
    lane = iota((16, 128), 1)
    row = iota((16, 128), 0)
    diag = (iota((128, 128), 0) == iota((128, 128), 1))
    z_from = iota((128, 128), 0)
    z_to = iota((128, 128), 1)
    difference = (
        jnp.where(z_from == z_to + 1, 1.0, 0.0) - jnp.where(z_from + 1 == z_to, 1.0, 0.0)
    ).astype(BF16)
    from_low = jnp.where(z_to == 0, -1.0, 0.0).astype(BF16)
    from_high = jnp.where(z_to == 127, 1.0, 0.0).astype(BF16)
    x_low = slab_in[lower, 24:40, :]
    x_low = jnp.where(me > 0, x_low, 0.0)
    x_high = slab_in[upper, 24:40, :]
    x_high = jnp.where(me < devices - 1, x_high, 0.0)
    before = jnp.where(step > 0, before_ref[0].astype(F32), x_low)
    after = jnp.where(step < pl.num_programs(0) - 1, after_ref[0].astype(F32), x_high)
    for c in range(cells):
        here = step * cells + c
        block = ref_ref[pl.ds(c * 8, 8)]
        flat = block.reshape(128, 128)
        low_line = z_faces[0, pl.ds(here, 1), :]
        high_line = z_faces[1, pl.ds(here, 1), :]
        low_diag = jnp.where(diag, low_line, 0.0).astype(BF16)
        high_diag = jnp.where(diag, high_line, 0.0).astype(BF16)
        grad_z = (
            jnp.dot(flat, difference, preferred_element_type=F32)
            + jnp.dot(low_diag, from_low, preferred_element_type=F32)
            + jnp.dot(high_diag, from_high, preferred_element_type=F32)
        )
        y_low = y_faces[0, pl.ds(pl.multiple_of(here * 8, 8), 8), :]
        y_high = y_faces[1, pl.ds(pl.multiple_of(here * 8, 8), 8), :]
        index_low = jnp.where(here > 0, here - 1, rows)
        index_high = jnp.where(here < rows - 1, here + 1, rows + 1)
        middle, to_low, to_high = [], [], []
        for k in range(3):
            own = field[pl.ds(k * EXT + here, 16, stride=height), :]
            middle.append(own)
            to_low.append(field[pl.ds(k * EXT + index_low, 16, stride=height), :] - own)
            to_high.append(field[pl.ds(k * EXT + index_high, 16, stride=height), :] - own)
        wide = [before if c == 0 else ref_ref[c * 8 - 1].astype(F32)]
        wide += [block[s].astype(F32) for s in range(8)]
        wide += [after if c == cells - 1 else ref_ref[c * 8 + 8].astype(F32)]
        for s in range(8):
            t = (s + 0.5) / 8.0 - 0.5
            side = to_low if t < 0 else to_high
            value = [middle[k] + abs(t) * side[k] for k in range(3)]
            own = wide[s + 1]
            y_up = jnp.where(row == 15, y_high[s : s + 1], roll(own, -1, 0))
            y_down = jnp.where(row == 0, y_low[s : s + 1], roll(own, 1, 0))
            total = def_ref[c * 8 + s].astype(F32) - own
            total = total - (wide[s + 2] - wide[s]) * value[0]
            total = total - (y_up - y_down) * value[1]
            total = total - grad_z[s * 16 : s * 16 + 16] * value[2]
            out_ref[c * 8 + s] = total.astype(BF16)


def solution(mesh):
    gx, gy, gz = (mesh.shape[a] for a in ("gx", "gy", "gz"))

    def pairs(even_up):
        out = []
        for y in range(gy):
            for z in range(gz):
                to = y + (1 if (z % 2 == 0) == even_up else -1)
                if 0 <= to < gy:
                    out.append((y * gz + z, to * gz + z))
        return out

    def on_device(ref_image, def_image, displacement):
        sizex, sizey, sizez = ref_image.shape
        rows = sizex // 8
        weights, table = solve_tables(gx, rows)
        chunk = 64
        steps = sizex // chunk
        disp = jnp.transpose(displacement, (0, 2, 3, 1))
        image_block = pl.BlockSpec((chunk, sizey, sizez), lambda i: (i, 0, 0))

        def whole(shape):
            return pl.BlockSpec(shape, lambda i: (0,) * len(shape))

        coarse_shape = (2, rows, 128)
        z_rows = 3 * rows + 32
        y_rows = 3 * rows + sizex
        coarse, up, down, y_high, y_low = pl.pallas_call(
            lambda *refs: bin_kernel(chunk, *refs),
            name="bin_and_pack",
            grid=(steps,),
            in_specs=[image_block, image_block, whole(disp.shape)],
            out_specs=[
                whole(coarse_shape), whole((z_rows, 128)), whole((z_rows, 128)),
                whole((sizex, 128)), whole((sizex, 128)),
            ],
            out_shape=[
                jax.ShapeDtypeStruct(coarse_shape, F32),
                jax.ShapeDtypeStruct((z_rows, 128), BF16),
                jax.ShapeDtypeStruct((z_rows, 128), BF16),
                jax.ShapeDtypeStruct((sizex, 128), BF16),
                jax.ShapeDtypeStruct((sizex, 128), BF16),
            ],
            scratch_shapes=[pltpu.VMEM((2, 2, rows, 128), F32), pltpu.VMEM((2, 32, 128), F32)],
        )(ref_image, def_image, disp)
        z_low = lax.ppermute(up, "gz", [(i, (i + 1) % gz) for i in range(gz)])
        z_high = lax.ppermute(down, "gz", [((i + 1) % gz, i) for i in range(gz)])
        coarse, first, second = pl.pallas_call(
            lambda *refs: z_kernel(gz, *refs),
            name="extend_along_z",
            in_specs=[VMEM] * 5,
            out_specs=[VMEM] * 3,
            out_shape=[
                jax.ShapeDtypeStruct(coarse_shape, F32),
                jax.ShapeDtypeStruct((y_rows, 128), BF16),
                jax.ShapeDtypeStruct((y_rows, 128), BF16),
            ],
        )(coarse, z_low, z_high, y_high, y_low)
        first = lax.ppermute(first, ("gy", "gz"), pairs(True))
        second = lax.ppermute(second, ("gy", "gz"), pairs(False))
        plane = (1, sizey, sizez)
        slabs, rhs, disp = pl.pallas_call(
            rhs_kernel,
            name="right_hand_sides",
            grid=(1,),
            in_specs=[
                whole(coarse_shape), whole((y_rows, 128)), whole((y_rows, 128)),
                pl.BlockSpec(plane, lambda i: (0, 0, 0)),
                pl.BlockSpec(plane, lambda i: (sizex - 1, 0, 0)),
                whole(weights.shape),
            ],
            out_specs=[
                whole((gx, SLAB, 128)), whole((3, rows, 128)), whole((3, rows, 128)),
            ],
            out_shape=[
                jax.ShapeDtypeStruct((gx, SLAB, 128), F32),
                jax.ShapeDtypeStruct((3, rows, 128), F32),
                jax.ShapeDtypeStruct((3, rows, 128), F32),
            ],
        )(coarse, first, second, ref_image, ref_image, jnp.asarray(weights))
        slabs = lax.all_to_all(slabs, "gx", 0, 0, tiled=True)
        z_block = pl.BlockSpec((32, 128), lambda i: (3, 0))
        new, residual = pl.pallas_call(
            lambda *refs: fine_kernel(
                chunk, *refs[:6],
                refs[6].at[pl.ds(3 * rows, sizex)], refs[7].at[pl.ds(3 * rows, sizex)],
                *refs[8:],
            ),
            name="solve_and_residual",
            grid=(steps,),
            in_specs=[
                whole((gx, SLAB, 128)), whole((3, rows, 128)), whole((3, rows, 128)),
                whole(table.shape), z_block, z_block,
                whole((y_rows, 128)), whole((y_rows, 128)),
                image_block,
                pl.BlockSpec(plane, lambda i: (jnp.maximum(i * chunk - 1, 0), 0, 0)),
                pl.BlockSpec(plane, lambda i: (jnp.minimum(i * chunk + chunk, sizex - 1), 0, 0)),
                image_block,
            ],
            out_specs=[whole((3, 2, 16, rows)), image_block],
            out_shape=[
                jax.ShapeDtypeStruct((3, 2, 16, rows), F32),
                jax.ShapeDtypeStruct(ref_image.shape, BF16),
            ],
            scratch_shapes=[
                pltpu.VMEM((16 * 3 * EXT, 128), F32),
                pltpu.VMEM((2, rows, 128), F32),
                pltpu.VMEM((2, sizex, 128), F32),
            ],
        )(
            slabs, rhs, disp, jnp.asarray(table), z_low, z_high, first, second,
            ref_image, ref_image, ref_image, def_image,
        )
        return jnp.transpose(new, (0, 3, 1, 2)), residual

    return jax.shard_map(
        on_device,
        mesh=mesh,
        in_specs=(P("gx", "gy", "gz"), P("gx", "gy", "gz"), P(None, "gx", "gy", "gz")),
        out_specs=(P(None, "gx", "gy", "gz"), P("gx", "gy", "gz")),
        check_vma=False,
    )
```

```python
import numpy as np
import jax
import jax.numpy as jnp
from jax import lax
from jax.experimental import pallas as pl
from jax.experimental.pallas import tpu as pltpu
from jax.sharding import PartitionSpec as P

STIFFNESS = 64.0
SPAN = 20
VMEM = pl.BlockSpec(memory_space=pltpu.VMEM)
HBM = pl.BlockSpec(memory_space=pltpu.HBM)
HIGHEST = lax.Precision.HIGHEST
F32 = jnp.float32
BF16 = jnp.bfloat16
SLAB = 48
VMEM_BYTES = 16 * 2**20
EXT = 40


def inverse_entry(lines):
    diagonal = 1.0 + 2.0 * STIFFNESS
    root = (diagonal - np.sqrt(diagonal**2 - 4.0 * STIFFNESS**2)) / (2.0 * STIFFNESS)
    theta = -np.log(root)
    scale = 1.0 / (2.0 * STIFFNESS * np.sinh(theta) * (1.0 - root ** (2.0 * (lines + 1))))

    def first(i):
        return 1.0 - root ** (2.0 * (i + 1))

    def last(i):
        return 1.0 - root ** (2.0 * (lines - i))

    return root, scale, first, last


def solve_tables(devices, cells):
    lines = devices * cells
    root, scale, first, last = inverse_entry(lines)
    local = np.arange(cells)
    weights = np.zeros((devices, 8, cells))
    table = np.zeros((devices, EXT, cells + 3 * devices))
    everyone = np.arange(devices)
    for p in range(devices):
        at = p * cells + local
        weights[p, 0] = first(at) * root ** (cells - 1.0 - local)
        weights[p, 1] = last(at) * root**local
        rows = np.concatenate([at, [p * cells - 1, p * cells + cells]])[:, None]
        used = slice(0, cells + 2)

        def entry(columns):
            low, high = np.minimum(rows, columns), np.maximum(rows, columns)
            return scale * root ** (1.0 * (high - low)) * first(low) * last(high)

        table[p, used, :cells] = entry(at[None, :])
        below, above = (everyone < p)[None, :], (everyone > p)[None, :]
        gap = np.where(below, rows - (everyone * cells + cells - 1)[None, :], 0)
        sums = below * last(rows) * root ** (1.0 * gap)
        gap = np.where(above, (everyone * cells)[None, :] - rows, 0)
        sums += above * first(rows) * root ** (1.0 * gap)
        table[p, used, cells : cells + devices] = scale * sums
        table[p, used, cells + devices : cells + 2 * devices] = entry((everyone * cells)[None, :])
        table[p, used, cells + 2 * devices :] = entry((everyone * cells + cells - 1)[None, :])
    return weights.astype(np.float32), table.astype(np.float32)


def prolong_table(sizey, sizez):
    lane = np.arange(128)[:, None]
    coarse_y, coarse_z = lane // SPAN - 1, lane % SPAN - 2

    def tent(fine, coarse):
        return np.maximum(1.0 - np.abs((fine + 0.5) / 8.0 - 0.5 - coarse), 0.0)

    along_y = tent(np.arange(sizey)[None, :], coarse_y) * (lane < 4 * SPAN)
    along_z = tent(np.arange(sizez)[None, :], coarse_z)
    product = 0.5 * along_y[:, :, None] * along_z[:, None, :]
    return product.reshape(128, sizey * sizez).astype(BF16)


def iota(shape, dim):
    return lax.broadcasted_iota(jnp.int32, shape, dim)


def roll(value, shift, axis):
    size = value.shape[axis]
    return pltpu.roll(value, shift % size, axis)


def exact_dot(a, b, dims):
    return lax.dot_general(a, b, (dims, ((), ())), precision=HIGHEST, preferred_element_type=F32)


def put_split(ref, start, value):
    rows = value.shape[0]
    for part in range(3):
        piece = value.astype(BF16)
        ref[pl.ds(start + part * rows, rows), :] = piece
        value = value - piece.astype(F32)


def get_split(ref, rows):
    return (
        ref[0:rows, :].astype(F32)
        + ref[rows : 2 * rows, :].astype(F32)
        + ref[2 * rows : 3 * rows, :].astype(F32)
    )


def bin_kernel(
    chunk, ref_hbm, def_hbm, disp_hbm,
    coarse_ref, up_ref, down_ref, y_high_ref, y_low_ref,
    ref_buf, def_buf, disp_buf, bins, faces, sems, disp_sem,
):
    cells = chunk // 8
    steps = ref_buf.shape[0] // chunk

    def copy(k, step):
        source, target = ((ref_hbm, ref_buf), (def_hbm, def_buf))[k]
        planes = pl.ds(step * chunk, chunk)
        return pltpu.make_async_copy(source.at[planes], target.at[planes], sems.at[k, step])

    disp_copy = pltpu.make_async_copy(disp_hbm, disp_buf, disp_sem)
    for step in range(steps):
        copy(0, step).start()
        copy(1, step).start()
    disp_copy.start()
    lane = iota((16, 128), 1)
    row = iota((16, 128), 0)
    pick = jnp.where(
        ((row == 0) & (lane == 127)) | ((row == 1) & (lane == 0)), 1.0, 0.0
    ).astype(BF16)
    for step in range(steps):
        x0, row0 = step * chunk, step * cells
        for k, image in enumerate((ref_buf, def_buf)):
            copy(k, step).wait()
            for c in range(cells):
                total = image[pl.ds(x0 + c * 8, 8)].astype(F32).sum(0)
                for y in range(2):
                    bins[k, y, row0 + c : row0 + c + 1, :] = total[y * 8 : y * 8 + 8].sum(
                        0, keepdims=True
                    )
        flat = ref_buf[pl.ds(x0, chunk)].reshape(chunk * 16, 128)
        sides = lax.dot_general(
            pick, flat, (((1,), (1,)), ((), ())), preferred_element_type=F32
        )
        for c in range(cells):
            at = row0 + c
            faces[0, at : at + 1, :] = sides[0:1, c * 128 : (c + 1) * 128]
            faces[1, at : at + 1, :] = sides[1:2, c * 128 : (c + 1) * 128]
        wide = ref_buf[pl.ds(x0, chunk)].astype(F32)
        y_high_ref[pl.ds(x0, chunk), :] = wide[:, 15, :].astype(BF16)
        y_low_ref[pl.ds(x0, chunk), :] = wide[:, 0, :].astype(BF16)
    disp_copy.wait()
    rows = bins.shape[2]
    z = iota((128, 128), 0) // 8
    lanes = iota((128, 128), 1)
    place_lanes = iota((16, 128), 1)
    place_z = iota((16, 128), 0)
    whole = []
    for y in range(2):
        total = jnp.zeros((rows, 128), F32)
        for k in range(2):
            summer = jnp.where(lanes == k * SPAN + 2 + z, 1.0 / 32.0, 0.0)
            total += exact_dot(bins[k, y], summer, ((1,), (0,)))
        for k in range(3):
            place = jnp.where(place_lanes == (2 + k) * SPAN + 2 + place_z, 1.0, 0.0)
            total += exact_dot(disp_buf[k, y], place, ((0,), (0,)))
        coarse_ref[y] = total
        whole.append(total)
    position = iota((rows, 128), 1) % SPAN
    up = jnp.where(position < 2, roll(whole[0], -16, 1), roll(whole[1], -12, 1))
    down = jnp.where(position >= 18, roll(whole[0], 16, 1), roll(whole[1], 12, 1))
    put_split(up_ref, 0, up)
    put_split(down_ref, 0, down)
    up_ref[pl.ds(3 * rows, 32), :] = faces[0].astype(BF16)
    down_ref[pl.ds(3 * rows, 32), :] = faces[1].astype(BF16)


def z_kernel(
    devices, coarse_in, low_in, high_in, y_high_in, y_low_in, coarse_out, down_out, up_out
):
    rows = coarse_in.shape[1]
    me = lax.axis_index("gz")
    lane = iota((rows, 128), 1)
    position = lane % SPAN
    inside = lane < 5 * SPAN
    low = jnp.where(me > 0, get_split(low_in, rows), 0.0)
    high = jnp.where(me < devices - 1, get_split(high_in, rows), 0.0)
    whole = []
    for y in range(2):
        value = coarse_in[y]
        value = jnp.where((position < 2) & inside, roll(low, -4 * y, 1), value)
        value = jnp.where((position >= 18) & inside, roll(high, 4 * y, 1), value)
        coarse_out[y] = value
        whole.append(value)
    up = jnp.where(inside, whole[1], roll(whole[0], 100, 1))
    down = jnp.where(inside, whole[0], roll(whole[1], 100, 1))
    put_split(down_out, 0, down)
    put_split(up_out, 0, up)
    fine = y_high_in.shape[0]
    down_out[pl.ds(3 * rows, fine), :] = y_low_in[...]
    up_out[pl.ds(3 * rows, fine), :] = y_high_in[...]


def rhs_kernel(
    coarse_in, above_in, below_in, ref_in, weights_in,
    slab_out, rhs_out, disp_out,
):
    rows = coarse_in.shape[1]
    devices = slab_out.shape[0]
    me = lax.axis_index("gx")
    below, above = get_split(below_in, rows), get_split(above_in, rows)
    layers = [below, coarse_in[0], coarse_in[1], above]
    lane = iota((rows, 128), 1)
    group = lane // SPAN
    position = lane % SPAN
    row = iota((rows, 128), 0)

    def packed(sources):
        value = jnp.zeros((rows, 128), F32)
        for y, (layer, at) in enumerate(sources):
            value = jnp.where(group == y, roll(layer, SPAN * y - at, 1), value)
        return value

    cell = packed([(layer, 0) for layer in layers])
    cell_below = packed([(below, 100), (layers[0], 0), (layers[1], 0), (layers[2], 0)])
    cell_above = packed([(layers[1], 0), (layers[2], 0), (layers[3], 0), (above, 100)])
    cell_def = packed([(layer, SPAN) for layer in layers])
    disp = [packed([(layer, (2 + k) * SPAN) for layer in layers]) for k in range(3)]
    slope_y = (cell_above - cell_below) * 0.5
    slope_z = (roll(cell, -1, 1) - roll(cell, 1, 1)) * 0.5
    slope_x = (roll(cell, -1, 0) - roll(cell, 1, 0)) * 0.5
    partial = cell_def - cell - (slope_y * disp[1] + slope_z * disp[2])
    mismatch = partial - slope_x * disp[0]
    keep = (position >= 1) & (position < SPAN - 1) & (row > 0) & (row < rows - 1)
    keep &= lane < 4 * SPAN
    weights = weights_in[me]
    sums = []
    for k, slope in enumerate((slope_x, slope_y, slope_z)):
        rhs = jnp.where(keep, slope * mismatch, 0.0)
        rhs_out[k] = rhs
        disp_out[k] = disp[k]
        sums.append(exact_dot(weights, rhs, ((1,), (0,))))
    end = rows - 1
    shared = [cell[i : i + 1] for i in (0, 1, end - 1, end)]
    shared += [partial[0:1], partial[end:], disp[0][0:1], disp[0][end:], slope_y[0:1]]
    shared_more = [slope_y[end:], slope_z[0:1], slope_z[end:]]
    zero = jnp.zeros((1, 128), F32)
    lane = iota((12, 128), 1)

    def message(sum_row, edge):
        main = jnp.concatenate([s[sum_row : sum_row + 1] for s in sums] + shared, axis=0)
        edges = [disp[1][edge : edge + 1], disp[2][edge : edge + 1], zero]
        more = jnp.concatenate(shared_more + edges, axis=0)
        more = jnp.concatenate([roll(more, 4 * SPAN, 1), roll(more, 2 * SPAN, 1)], axis=0)
        rest = jnp.where(lane < 4 * SPAN, main, more)
        pieces = []
        for _ in range(3):
            piece = rest.astype(BF16).astype(F32)
            pieces.append(piece)
            rest = rest - piece
        return jnp.concatenate([pieces[0], pieces[1], pieces[2][:8]], axis=0).astype(BF16)

    to_above, to_below = message(0, end), message(1, 0)
    low_plane, high_plane = ref_in[0], ref_in[ref_in.shape[0] - 1]
    for q in range(devices):
        slab_out[q, 0:16, :] = jnp.where(me > q, low_plane, high_plane)
        slab_out[q, 16:48, :] = jnp.where(me > q, to_below, to_above)


def fine_kernel(
    slab_in, rhs_in, disp_in, table_in, prolong_in, z_low_in, z_high_in, above_in, below_in,
    ref_in, def_in,
    disp_out, out_hbm,
    lines, field, z_faces, out_buf, sems,
):
    devices = slab_in.shape[0]
    rows = rhs_in.shape[1]
    me = lax.axis_index("gx")
    me_z = lax.axis_index("gz")
    last_z = lax.axis_size("gz") - 1
    height = 3 * EXT
    lines[...] = slab_in[:, 16:48, :].astype(F32)
    lane = iota((devices, 128), 1)
    q = iota((devices, 128), 0)
    keep = (lane % SPAN >= 1) & (lane % SPAN < SPAN - 1) & (lane < 4 * SPAN)

    def whole_line(i):
        value = lines[:, i, :] + lines[:, 12 + i, :]
        return value + lines[:, 24 + i, :] if i < 8 else value

    full = [whole_line(i) for i in range(12)]
    more = [
        jnp.where(lane < 2 * SPAN, roll(full[i], -4 * SPAN, 1), roll(full[6 + i], -2 * SPAN, 1))
        for i in range(5)
    ]
    cell_0, cell_1, cell_30, cell_31 = full[3:7]
    from_below = jnp.where(q > 0, roll(cell_31, 1, 0), 0.0)
    from_above = jnp.where(q < devices - 1, roll(cell_0, -1, 0), 0.0)
    slopes_0 = ((cell_1 - from_below) * 0.5, full[11], more[1])
    slopes_1 = ((from_above - cell_30) * 0.5, more[0], more[2])
    mismatch_0 = full[7] - slopes_0[0] * full[9]
    mismatch_1 = full[8] - slopes_1[0] * full[10]
    known = []
    for k in range(3):
        edge_0 = jnp.where(keep, slopes_0[k] * mismatch_0, 0.0)
        edge_1 = jnp.where(keep, slopes_1[k] * mismatch_1, 0.0)
        known.append(jnp.concatenate([rhs_in[k], full[k], edge_0, edge_1], axis=0))
    moved = exact_dot(table_in[me], jnp.concatenate(known, axis=1), ((1,), (0,)))

    def one(value, at):
        return jnp.where(q == at, value, 0.0).sum(0, keepdims=True)

    edge = iota((EXT - rows, 128), 0)
    block_lane = iota((EXT, 128), 1)
    block_keep = (block_lane % SPAN >= 1) & (block_lane % SPAN < SPAN - 1)
    block_keep &= block_lane < 4 * SPAN
    solved, inner = [], []
    for k in range(3):
        low_row = one((full[10], more[3], more[4])[k], me - 1)
        high_row = one((full[9], more[3], more[4])[k], me + 1)
        outer = jnp.where(edge == 0, low_row, jnp.where(edge == 1, high_row, 0.0))
        before = jnp.concatenate([disp_in[k], outer], axis=0)
        after = jnp.where(block_keep, before + moved[:, k * 128 : k * 128 + 128], 0.0)
        solved.append(after)
        inner.append(after[:rows])
    whole = jnp.concatenate(solved, axis=0)
    high = whole.astype(BF16)
    low = (whole - high.astype(F32)).astype(BF16)
    for y in range(0, 16, 2):
        table = prolong_in[:, y * 128 : y * 128 + 256]
        product = jnp.dot(high, table, preferred_element_type=F32) + jnp.dot(
            low, table, preferred_element_type=F32
        )
        field[y * height : (y + 1) * height, :] = product[:, :128]
        field[(y + 1) * height : (y + 2) * height, :] = product[:, 128:]
    own_lane, own_row = iota((32, 128), 1), iota((32, 128), 0)
    pick = jnp.where(own_lane == SPAN * (own_row // 16 + 1) + 2 + own_row % 16, 1.0, 0.0)
    placed = exact_dot(pick, jnp.concatenate(inner, axis=0), ((1,), (1,)))
    for k in range(3):
        for y in range(2):
            disp_out[k, y] = placed[16 * y : 16 * y + 16, k * rows : (k + 1) * rows]

    z_faces[0] = jnp.where(me_z > 0, z_low_in[3 * rows :, :].astype(F32), 0.0)
    z_faces[1] = jnp.where(me_z < last_z, z_high_in[3 * rows :, :].astype(F32), 0.0)
    eye = jnp.where(iota((128, 128), 0) == iota((128, 128), 1), 1.0, 0.0).astype(BF16)
    z_from, z_to = iota((384, 128), 0), iota((384, 128), 1)
    z_table = jnp.where((z_from == z_to + 1) & (z_from < 128), 1.0, 0.0)
    z_table -= jnp.where(z_from + 1 == z_to, 1.0, 0.0)
    z_table -= jnp.where((z_from >= 128) & (z_from < 256) & (z_to == 0), 1.0, 0.0)
    z_table += jnp.where((z_from >= 256) & (z_to == 127), 1.0, 0.0)
    z_table = z_table.astype(BF16)
    y_to, y_from = iota((128, 160), 0), iota((128, 160), 1)
    y_tables = []
    for half in range(2):
        low_at = 128 + 8 * half + y_to // 16
        plus = jnp.where(y_to % 16 == 15, low_at + 16, y_to + 1)
        minus = jnp.where(y_to % 16 == 0, low_at, y_to - 1)
        y_table = jnp.where(y_from == plus, 1.0, 0.0) - jnp.where(y_from == minus, 1.0, 0.0)
        y_tables.append(y_table.astype(BF16))
    x_low = slab_in[jnp.maximum(me - 1, 0), 0:16, :].astype(F32)
    x_low = jnp.where(me > 0, x_low, 0.0)
    x_high = slab_in[jnp.minimum(me + 1, devices - 1), 0:16, :].astype(F32)
    x_high = jnp.where(me < devices - 1, x_high, 0.0)
    cells = 4
    sizex = ref_in.shape[0]
    steps = rows // cells

    def send(step):
        planes = pl.ds(step * cells * 8, cells * 8)
        return pltpu.make_async_copy(out_buf.at[planes], out_hbm.at[planes], sems.at[step])

    def body(step, _):
        x0 = step * (cells * 8)
        before = ref_in[jnp.maximum(x0 - 1, 0)].astype(F32)
        before = jnp.where(step > 0, before, x_low)
        after = ref_in[jnp.minimum(x0 + cells * 8, sizex - 1)].astype(F32)
        after = jnp.where(step < steps - 1, after, x_high)
        y_rows = pl.ds(pl.multiple_of(3 * rows + x0, 32), cells * 8)
        y_lows = below_in[y_rows, :]
        y_highs = above_in[y_rows, :]
        index_low = jnp.where(step > 0, step * cells - 1, rows)
        index_high = jnp.where(step < steps - 1, step * cells + cells, rows + 1)
        indices = [index_low] + [step * cells + c for c in range(cells)] + [index_high]
        nodes = [
            [field[pl.ds(k * EXT + i, 16, stride=height), :] for k in range(3)] for i in indices
        ]
        slope = [(nodes[1][k] - nodes[0][k]) * 0.125 for k in range(3)]
        for c in range(cells):
            here = step * cells + c
            block = ref_in[pl.ds(x0 + c * 8, 8)]
            flat = block.reshape(128, 128)
            low_line = jnp.broadcast_to(z_faces[0, pl.ds(here, 1), :], (16, 128)).astype(BF16)
            high_line = jnp.broadcast_to(z_faces[1, pl.ds(here, 1), :], (16, 128)).astype(BF16)
            grad_z = jnp.dot(
                jnp.concatenate(
                    [
                        flat,
                        eye * jnp.concatenate([low_line] * 8, axis=0),
                        eye * jnp.concatenate([high_line] * 8, axis=0),
                    ],
                    axis=1,
                ),
                z_table,
                preferred_element_type=F32,
            )
            pair = slice(c // 2 * 16, c // 2 * 16 + 16)
            grad_y = jnp.dot(
                y_tables[c % 2],
                jnp.concatenate([flat, y_lows[pair], y_highs[pair]], axis=0),
                preferred_element_type=F32,
            )
            next_slope = [(nodes[c + 2][k] - nodes[c + 1][k]) * 0.125 for k in range(3)]
            wide = [before if c == 0 else ref_in[x0 + c * 8 - 1].astype(F32)]
            wide += [block[s].astype(F32) for s in range(8)]
            wide += [after if c == cells - 1 else ref_in[x0 + c * 8 + 8].astype(F32)]
            for s in range(8):
                if s == 0:
                    value = [nodes[c + 1][k] - 3.5 * slope[k] for k in range(3)]
                elif s == 4:
                    slope = next_slope
                    value = [nodes[c + 1][k] + 0.5 * slope[k] for k in range(3)]
                else:
                    value = [value[k] + slope[k] for k in range(3)]
                line = c * 8 + s
                rows_s = slice(s * 16, s * 16 + 16)
                total = def_in[x0 + line].astype(F32) - wide[s + 1]
                total = total - (wide[s + 2] - wide[s]) * value[0]
                total = total - grad_y[rows_s] * value[1]
                total = total - grad_z[rows_s] * value[2]
                out_buf[x0 + line] = total.astype(BF16)
        send(step).start()
        return 0

    lax.fori_loop(0, steps, body, 0)
    for step in range(steps):
        send(step).wait()


def solution(mesh):
    gx, gy, gz = (mesh.shape[a] for a in ("gx", "gy", "gz"))

    def on_device(ref_image, def_image, displacement):
        sizex, sizey, sizez = ref_image.shape
        rows = sizex // 8
        weights, table = solve_tables(gx, rows)
        chunk = 64
        disp = jnp.transpose(displacement, (0, 2, 3, 1))
        coarse_shape = (2, rows, 128)
        z_rows = 3 * rows + 32
        y_rows = 3 * rows + sizex
        params = pltpu.CompilerParams(vmem_limit_bytes=VMEM_BYTES)
        coarse, up, down, y_high, y_low = pl.pallas_call(
            lambda *refs: bin_kernel(chunk, *refs),
            name="bin_and_pack",
            in_specs=[HBM] * 3,
            out_specs=[VMEM] * 5,
            out_shape=[
                jax.ShapeDtypeStruct(coarse_shape, F32),
                jax.ShapeDtypeStruct((z_rows, 128), BF16),
                jax.ShapeDtypeStruct((z_rows, 128), BF16),
                jax.ShapeDtypeStruct((sizex, 128), BF16),
                jax.ShapeDtypeStruct((sizex, 128), BF16),
            ],
            scratch_shapes=[
                pltpu.VMEM(ref_image.shape, BF16),
                pltpu.VMEM(def_image.shape, BF16),
                pltpu.VMEM(disp.shape, F32),
                pltpu.VMEM((2, 2, rows, 128), F32),
                pltpu.VMEM((2, 32, 128), F32),
                pltpu.SemaphoreType.DMA((2, sizex // chunk)),
                pltpu.SemaphoreType.DMA,
            ],
            compiler_params=params,
        )(ref_image, def_image, disp)
        z_low = lax.ppermute(up, "gz", [(i, (i + 1) % gz) for i in range(gz)])
        z_high = lax.ppermute(down, "gz", [((i + 1) % gz, i) for i in range(gz)])
        coarse, down, up = pl.pallas_call(
            lambda *refs: z_kernel(gz, *refs),
            name="extend_along_z",
            in_specs=[VMEM] * 5,
            out_specs=[VMEM] * 3,
            out_shape=[
                jax.ShapeDtypeStruct(coarse_shape, F32),
                jax.ShapeDtypeStruct((y_rows, 128), BF16),
                jax.ShapeDtypeStruct((y_rows, 128), BF16),
            ],
            compiler_params=params,
        )(coarse, z_low, z_high, y_high, y_low)
        above = lax.ppermute(down, "gy", [(i + 1, i) for i in range(gy - 1)])
        below = lax.ppermute(up, "gy", [(i, i + 1) for i in range(gy - 1)])
        slabs, rhs, disp = pl.pallas_call(
            rhs_kernel,
            name="right_hand_sides",
            in_specs=[VMEM] * 5,
            out_specs=[VMEM] * 3,
            out_shape=[
                jax.ShapeDtypeStruct((gx, SLAB, 128), BF16),
                jax.ShapeDtypeStruct((3, rows, 128), F32),
                jax.ShapeDtypeStruct((3, rows, 128), F32),
            ],
            compiler_params=params,
        )(coarse, above, below, ref_image, jnp.asarray(weights))
        slabs = lax.all_to_all(slabs, "gx", 0, 0, tiled=True)
        new, residual = pl.pallas_call(
            fine_kernel,
            name="solve_and_residual",
            in_specs=[VMEM] * 11,
            out_specs=[VMEM, HBM],
            out_shape=[
                jax.ShapeDtypeStruct((3, 2, 16, rows), F32),
                jax.ShapeDtypeStruct(ref_image.shape, BF16),
            ],
            scratch_shapes=[
                pltpu.VMEM((gx, 32, 128), F32),
                pltpu.VMEM((16 * 3 * EXT, 128), F32),
                pltpu.VMEM((2, rows, 128), F32),
                pltpu.VMEM(ref_image.shape, BF16),
                pltpu.SemaphoreType.DMA((rows // 4,)),
            ],
            compiler_params=params,
        )(
            slabs, rhs, disp, jnp.asarray(table), jnp.asarray(prolong_table(sizey, sizez)),
            z_low, z_high, above, below, ref_image, def_image,
        )
        return jnp.transpose(new, (0, 3, 1, 2)), residual

    return jax.shard_map(
        on_device,
        mesh=mesh,
        in_specs=(P("gx", "gy", "gz"), P("gx", "gy", "gz"), P(None, "gx", "gy", "gz")),
        out_specs=(P(None, "gx", "gy", "gz"), P("gx", "gy", "gz")),
        check_vma=False,
    )
```

```python
import numpy as np
import jax
import jax.numpy as jnp
from jax import lax
from jax.experimental import pallas as pl
from jax.experimental.pallas import tpu as pltpu
from jax.sharding import PartitionSpec as P

STIFFNESS = 64.0
SPAN = 20
VMEM = pl.BlockSpec(memory_space=pltpu.VMEM)
HBM = pl.BlockSpec(memory_space=pltpu.HBM)
HIGHEST = lax.Precision.HIGHEST
F32 = jnp.float32
BF16 = jnp.bfloat16
SLAB = 48
VMEM_BYTES = 16 * 2**20
FIRST_VMEM_BYTES = 54400 * 2**10
EXT = 40


def inverse_entry(lines):
    diagonal = 1.0 + 2.0 * STIFFNESS
    root = (diagonal - np.sqrt(diagonal**2 - 4.0 * STIFFNESS**2)) / (2.0 * STIFFNESS)
    theta = -np.log(root)
    scale = 1.0 / (2.0 * STIFFNESS * np.sinh(theta) * (1.0 - root ** (2.0 * (lines + 1))))

    def first(i):
        return 1.0 - root ** (2.0 * (i + 1))

    def last(i):
        return 1.0 - root ** (2.0 * (lines - i))

    return root, scale, first, last


def solve_tables(devices, cells):
    lines = devices * cells
    root, scale, first, last = inverse_entry(lines)
    local = np.arange(cells)
    weights = np.zeros((devices, 8, cells))
    table = np.zeros((devices, EXT, cells + 3 * devices))
    everyone = np.arange(devices)
    for p in range(devices):
        at = p * cells + local
        weights[p, 0] = first(at) * root ** (cells - 1.0 - local)
        weights[p, 1] = last(at) * root**local
        rows = np.concatenate([at, [p * cells - 1, p * cells + cells]])[:, None]
        used = slice(0, cells + 2)

        def entry(columns):
            low, high = np.minimum(rows, columns), np.maximum(rows, columns)
            return scale * root ** (1.0 * (high - low)) * first(low) * last(high)

        table[p, used, :cells] = entry(at[None, :])
        below, above = (everyone < p)[None, :], (everyone > p)[None, :]
        gap = np.where(below, rows - (everyone * cells + cells - 1)[None, :], 0)
        sums = below * last(rows) * root ** (1.0 * gap)
        gap = np.where(above, (everyone * cells)[None, :] - rows, 0)
        sums += above * first(rows) * root ** (1.0 * gap)
        table[p, used, cells : cells + devices] = scale * sums
        table[p, used, cells + devices : cells + 2 * devices] = entry((everyone * cells)[None, :])
        table[p, used, cells + 2 * devices :] = entry((everyone * cells + cells - 1)[None, :])
    return weights.astype(np.float32), table.astype(np.float32)


def prolong_table(sizey, sizez):
    lane = np.arange(128)[:, None]
    coarse_y, coarse_z = lane // SPAN - 1, lane % SPAN - 2

    def tent(fine, coarse):
        return np.maximum(1.0 - np.abs((fine + 0.5) / 8.0 - 0.5 - coarse), 0.0)

    along_y = tent(np.arange(sizey)[None, :], coarse_y) * (lane < 4 * SPAN)
    along_z = tent(np.arange(sizez)[None, :], coarse_z)
    product = 0.5 * along_y[:, :, None] * along_z[:, None, :]
    return product.reshape(128, sizey * sizez).astype(BF16)


def iota(shape, dim):
    return lax.broadcasted_iota(jnp.int32, shape, dim)


def roll(value, shift, axis):
    size = value.shape[axis]
    return pltpu.roll(value, shift % size, axis)


def exact_dot(a, b, dims):
    return lax.dot_general(a, b, (dims, ((), ())), precision=HIGHEST, preferred_element_type=F32)


def put_split(ref, start, value):
    rows = value.shape[0]
    for part in range(3):
        piece = value.astype(BF16)
        ref[pl.ds(start + part * rows, rows), :] = piece
        value = value - piece.astype(F32)


def get_split(ref, rows):
    return (
        ref[0:rows, :].astype(F32)
        + ref[rows : 2 * rows, :].astype(F32)
        + ref[2 * rows : 3 * rows, :].astype(F32)
    )


def bin_kernel(
    chunk, ref_hbm, def_hbm, disp_hbm,
    coarse_ref, up_ref, down_ref, y_high_ref, y_low_ref,
    ref_buf, def_buf, disp_buf, bins, faces, sems, disp_sem,
):
    cells = chunk // 8
    steps = ref_buf.shape[0] // chunk

    def copy(k, step):
        source, target = ((ref_hbm, ref_buf), (def_hbm, def_buf))[k]
        planes = pl.ds(step * chunk, chunk)
        return pltpu.make_async_copy(source.at[planes], target.at[planes], sems.at[k, step])

    disp_copy = pltpu.make_async_copy(disp_hbm, disp_buf, disp_sem)
    for step in range(steps):
        copy(0, step).start()
        copy(1, step).start()
    disp_copy.start()
    lane = iota((16, 128), 1)
    row = iota((16, 128), 0)
    pick = jnp.where(
        ((row == 0) & (lane == 127)) | ((row == 1) & (lane == 0)), 1.0, 0.0
    ).astype(BF16)
    for step in range(steps):
        x0, row0 = step * chunk, step * cells
        for k, image in enumerate((ref_buf, def_buf)):
            copy(k, step).wait()
            for c in range(cells):
                total = image[pl.ds(x0 + c * 8, 8)].astype(F32).sum(0)
                for y in range(2):
                    bins[k, y, row0 + c : row0 + c + 1, :] = total[y * 8 : y * 8 + 8].sum(
                        0, keepdims=True
                    )
        flat = ref_buf[pl.ds(x0, chunk)].reshape(chunk * 16, 128)
        sides = lax.dot_general(
            pick, flat, (((1,), (1,)), ((), ())), preferred_element_type=F32
        )
        for c in range(cells):
            at = row0 + c
            faces[0, at : at + 1, :] = sides[0:1, c * 128 : (c + 1) * 128]
            faces[1, at : at + 1, :] = sides[1:2, c * 128 : (c + 1) * 128]
        wide = ref_buf[pl.ds(x0, chunk)].astype(F32)
        y_high_ref[pl.ds(x0, chunk), :] = wide[:, 15, :].astype(BF16)
        y_low_ref[pl.ds(x0, chunk), :] = wide[:, 0, :].astype(BF16)
    disp_copy.wait()
    rows = bins.shape[2]
    z = iota((128, 128), 0) // 8
    lanes = iota((128, 128), 1)
    place_lanes = iota((16, 128), 1)
    place_z = iota((16, 128), 0)
    whole = []
    for y in range(2):
        total = jnp.zeros((rows, 128), F32)
        for k in range(2):
            summer = jnp.where(lanes == k * SPAN + 2 + z, 1.0 / 32.0, 0.0)
            total += exact_dot(bins[k, y], summer, ((1,), (0,)))
        for k in range(3):
            place = jnp.where(place_lanes == (2 + k) * SPAN + 2 + place_z, 1.0, 0.0)
            total += exact_dot(disp_buf[k, y], place, ((0,), (0,)))
        coarse_ref[y] = total
        whole.append(total)
    position = iota((rows, 128), 1) % SPAN
    up = jnp.where(position < 2, roll(whole[0], -16, 1), roll(whole[1], -12, 1))
    down = jnp.where(position >= 18, roll(whole[0], 16, 1), roll(whole[1], 12, 1))
    put_split(up_ref, 0, up)
    put_split(down_ref, 0, down)
    up_ref[pl.ds(3 * rows, 32), :] = faces[0].astype(BF16)
    down_ref[pl.ds(3 * rows, 32), :] = faces[1].astype(BF16)


def z_kernel(
    devices, coarse_in, low_in, high_in, y_high_in, y_low_in, coarse_out, down_out, up_out
):
    rows = coarse_in.shape[1]
    me = lax.axis_index("gz")
    lane = iota((rows, 128), 1)
    position = lane % SPAN
    inside = lane < 5 * SPAN
    low = jnp.where(me > 0, get_split(low_in, rows), 0.0)
    high = jnp.where(me < devices - 1, get_split(high_in, rows), 0.0)
    whole = []
    for y in range(2):
        value = coarse_in[y]
        value = jnp.where((position < 2) & inside, roll(low, -4 * y, 1), value)
        value = jnp.where((position >= 18) & inside, roll(high, 4 * y, 1), value)
        coarse_out[y] = value
        whole.append(value)
    up = jnp.where(inside, whole[1], roll(whole[0], 100, 1))
    down = jnp.where(inside, whole[0], roll(whole[1], 100, 1))
    put_split(down_out, 0, down)
    put_split(up_out, 0, up)
    fine = y_high_in.shape[0]
    down_out[pl.ds(3 * rows, fine), :] = y_low_in[...]
    up_out[pl.ds(3 * rows, fine), :] = y_high_in[...]


def rhs_kernel(
    coarse_in, above_in, below_in, ref_in, weights_in, _,
    slab_out, rhs_out, disp_out,
):
    rows = coarse_in.shape[1]
    devices = slab_out.shape[0]
    me = lax.axis_index("gx")
    below, above = get_split(below_in, rows), get_split(above_in, rows)
    layers = [below, coarse_in[0], coarse_in[1], above]
    lane = iota((rows, 128), 1)
    group = lane // SPAN
    position = lane % SPAN
    row = iota((rows, 128), 0)

    def packed(sources):
        value = jnp.zeros((rows, 128), F32)
        for y, (layer, at) in enumerate(sources):
            value = jnp.where(group == y, roll(layer, SPAN * y - at, 1), value)
        return value

    cell = packed([(layer, 0) for layer in layers])
    cell_below = packed([(below, 100), (layers[0], 0), (layers[1], 0), (layers[2], 0)])
    cell_above = packed([(layers[1], 0), (layers[2], 0), (layers[3], 0), (above, 100)])
    cell_def = packed([(layer, SPAN) for layer in layers])
    disp = [packed([(layer, (2 + k) * SPAN) for layer in layers]) for k in range(3)]
    slope_y = (cell_above - cell_below) * 0.5
    slope_z = (roll(cell, -1, 1) - roll(cell, 1, 1)) * 0.5
    slope_x = (roll(cell, -1, 0) - roll(cell, 1, 0)) * 0.5
    partial = cell_def - cell - (slope_y * disp[1] + slope_z * disp[2])
    mismatch = partial - slope_x * disp[0]
    keep = (position >= 1) & (position < SPAN - 1) & (row > 0) & (row < rows - 1)
    keep &= lane < 4 * SPAN
    weights = weights_in[me]
    sums = []
    for k, slope in enumerate((slope_x, slope_y, slope_z)):
        rhs = jnp.where(keep, slope * mismatch, 0.0)
        rhs_out[k] = rhs
        disp_out[k] = disp[k]
        sums.append(exact_dot(weights, rhs, ((1,), (0,))))
    end = rows - 1
    shared = [cell[i : i + 1] for i in (0, 1, end - 1, end)]
    shared += [partial[0:1], partial[end:], disp[0][0:1], disp[0][end:], slope_y[0:1]]
    shared_more = [slope_y[end:], slope_z[0:1], slope_z[end:]]
    zero = jnp.zeros((1, 128), F32)
    lane = iota((12, 128), 1)

    def message(sum_row, edge):
        main = jnp.concatenate([s[sum_row : sum_row + 1] for s in sums] + shared, axis=0)
        edges = [disp[1][edge : edge + 1], disp[2][edge : edge + 1], zero]
        more = jnp.concatenate(shared_more + edges, axis=0)
        more = jnp.concatenate([roll(more, 4 * SPAN, 1), roll(more, 2 * SPAN, 1)], axis=0)
        rest = jnp.where(lane < 4 * SPAN, main, more)
        pieces = []
        for _ in range(3):
            piece = rest.astype(BF16).astype(F32)
            pieces.append(piece)
            rest = rest - piece
        return jnp.concatenate([pieces[0], pieces[1], pieces[2][:8]], axis=0).astype(BF16)

    to_above, to_below = message(0, end), message(1, 0)
    low_plane, high_plane = ref_in[0], ref_in[ref_in.shape[0] - 1]
    for q in range(devices):
        slab_out[q, 0:16, :] = jnp.where(me > q, low_plane, high_plane)
        slab_out[q, 16:48, :] = jnp.where(me > q, to_below, to_above)


def gradient_kernel(
    z_low_in, z_high_in, ref_in, slopes, z_faces
):
    sizex = ref_in.shape[0]
    rows = sizex // 8
    me_z = lax.axis_index("gz")
    last_z = lax.axis_size("gz") - 1
    z_faces[0] = jnp.where(me_z > 0, z_low_in[3 * rows :, :].astype(F32), 0.0)
    z_faces[1] = jnp.where(me_z < last_z, z_high_in[3 * rows :, :].astype(F32), 0.0)
    eye = jnp.where(iota((128, 128), 0) == iota((128, 128), 1), 1.0, 0.0).astype(BF16)
    z_from, z_to = iota((384, 128), 0), iota((384, 128), 1)
    z_table = jnp.where((z_from == z_to + 1) & (z_from < 128), 1.0, 0.0)
    z_table -= jnp.where(z_from + 1 == z_to, 1.0, 0.0)
    z_table -= jnp.where((z_from >= 128) & (z_from < 256) & (z_to == 0), 1.0, 0.0)
    z_table += jnp.where((z_from >= 256) & (z_to == 127), 1.0, 0.0)
    z_table = z_table.astype(BF16)
    y_to, y_from = iota((128, 128), 0), iota((128, 128), 1)
    y_table = jnp.where((y_from == y_to + 1) & (y_to % 16 != 15), 1.0, 0.0)
    y_table -= jnp.where((y_from + 1 == y_to) & (y_to % 16 != 0), 1.0, 0.0)
    y_table = y_table.astype(BF16)
    cells = 4
    steps = rows // cells

    def body(step, _):
        x0 = step * (cells * 8)
        for c in range(cells):
            here = step * cells + c
            block = ref_in[pl.ds(x0 + c * 8, 8)]
            flat = block.reshape(128, 128)
            low_line = jnp.broadcast_to(z_faces[0, pl.ds(here, 1), :], (16, 128)).astype(BF16)
            high_line = jnp.broadcast_to(z_faces[1, pl.ds(here, 1), :], (16, 128)).astype(BF16)
            grad_z = jnp.dot(
                jnp.concatenate(
                    [
                        flat,
                        eye * jnp.concatenate([low_line] * 8, axis=0),
                        eye * jnp.concatenate([high_line] * 8, axis=0),
                    ],
                    axis=1,
                ),
                z_table,
                preferred_element_type=F32,
            )
            grad_y = jnp.dot(y_table, flat, preferred_element_type=F32)
            planes = pl.ds(x0 + c * 8, 8)
            slopes[0, planes] = grad_y.reshape(8, 16, 128)
            slopes[1, planes] = grad_z.reshape(8, 16, 128)
        return 0

    lax.fori_loop(0, steps, body, 0)


def fine_kernel(
    slab_in, rhs_in, disp_in, table_in, prolong_in, slopes, above_in, below_in, ref_in, def_in,
    disp_out, out_hbm,
    lines, field, out_buf, sems,
):
    cells = 4
    sizex = ref_in.shape[0]
    steps = sizex // (8 * cells)

    devices = slab_in.shape[0]
    rows = rhs_in.shape[1]
    me = lax.axis_index("gx")
    height = 3 * EXT
    lines[...] = slab_in[:, 16:48, :].astype(F32)
    lane = iota((devices, 128), 1)
    q = iota((devices, 128), 0)
    keep = (lane % SPAN >= 1) & (lane % SPAN < SPAN - 1) & (lane < 4 * SPAN)

    def whole_line(i):
        value = lines[:, i, :] + lines[:, 12 + i, :]
        return value + lines[:, 24 + i, :] if i < 8 else value

    full = [whole_line(i) for i in range(12)]
    more = [
        jnp.where(lane < 2 * SPAN, roll(full[i], -4 * SPAN, 1), roll(full[6 + i], -2 * SPAN, 1))
        for i in range(5)
    ]
    cell_0, cell_1, cell_30, cell_31 = full[3:7]
    from_below = jnp.where(q > 0, roll(cell_31, 1, 0), 0.0)
    from_above = jnp.where(q < devices - 1, roll(cell_0, -1, 0), 0.0)
    slopes_0 = ((cell_1 - from_below) * 0.5, full[11], more[1])
    slopes_1 = ((from_above - cell_30) * 0.5, more[0], more[2])
    mismatch_0 = full[7] - slopes_0[0] * full[9]
    mismatch_1 = full[8] - slopes_1[0] * full[10]
    known = []
    for k in range(3):
        edge_0 = jnp.where(keep, slopes_0[k] * mismatch_0, 0.0)
        edge_1 = jnp.where(keep, slopes_1[k] * mismatch_1, 0.0)
        known.append(jnp.concatenate([rhs_in[k], full[k], edge_0, edge_1], axis=0))
    moved = exact_dot(table_in[me], jnp.concatenate(known, axis=1), ((1,), (0,)))

    def one(value, at):
        return jnp.where(q == at, value, 0.0).sum(0, keepdims=True)

    edge = iota((EXT - rows, 128), 0)
    block_lane = iota((EXT, 128), 1)
    block_keep = (block_lane % SPAN >= 1) & (block_lane % SPAN < SPAN - 1)
    block_keep &= block_lane < 4 * SPAN
    solved, inner = [], []
    for k in range(3):
        low_row = one((full[10], more[3], more[4])[k], me - 1)
        high_row = one((full[9], more[3], more[4])[k], me + 1)
        outer = jnp.where(edge == 0, low_row, jnp.where(edge == 1, high_row, 0.0))
        before = jnp.concatenate([disp_in[k], outer], axis=0)
        after = jnp.where(block_keep, before + moved[:, k * 128 : k * 128 + 128], 0.0)
        solved.append(after)
        inner.append(after[:rows])
    whole = jnp.concatenate(solved, axis=0)
    high = whole.astype(BF16)
    low = (whole - high.astype(F32)).astype(BF16)
    for y in range(0, 16, 2):
        table = prolong_in[:, y * 128 : y * 128 + 256]
        product = jnp.dot(high, table, preferred_element_type=F32) + jnp.dot(
            low, table, preferred_element_type=F32
        )
        field[y * height : (y + 1) * height, :] = product[:, :128]
        field[(y + 1) * height : (y + 2) * height, :] = product[:, 128:]
    own_lane, own_row = iota((32, 128), 1), iota((32, 128), 0)
    pick = jnp.where(own_lane == SPAN * (own_row // 16 + 1) + 2 + own_row % 16, 1.0, 0.0)
    placed = exact_dot(pick, jnp.concatenate(inner, axis=0), ((1,), (1,)))
    for k in range(3):
        for y in range(2):
            disp_out[k, y] = placed[16 * y : 16 * y + 16, k * rows : (k + 1) * rows]

    x_low = slab_in[jnp.maximum(me - 1, 0), 0:16, :].astype(F32)
    x_low = jnp.where(me > 0, x_low, 0.0)
    x_high = slab_in[jnp.minimum(me + 1, devices - 1), 0:16, :].astype(F32)
    x_high = jnp.where(me < devices - 1, x_high, 0.0)
    row = iota((16, 128), 0)

    def send(step):
        planes = pl.ds(step * cells * 8, cells * 8)
        return pltpu.make_async_copy(out_buf.at[planes], out_hbm.at[planes], sems.at[step])

    def body(step, _):
        x0 = step * (cells * 8)
        y_rows = pl.ds(pl.multiple_of(3 * rows + x0, 32), cells * 8)
        y_lows = below_in[y_rows, :].astype(F32)
        y_highs = above_in[y_rows, :].astype(F32)
        before = ref_in[jnp.maximum(x0 - 1, 0)].astype(F32)
        before = jnp.where(step > 0, before, x_low)
        after = ref_in[jnp.minimum(x0 + cells * 8, sizex - 1)].astype(F32)
        after = jnp.where(step < steps - 1, after, x_high)
        index_low = jnp.where(step > 0, step * cells - 1, rows)
        index_high = jnp.where(step < steps - 1, step * cells + cells, rows + 1)
        indices = [index_low] + [step * cells + c for c in range(cells)] + [index_high]
        nodes = [
            [field[pl.ds(k * EXT + i, 16, stride=height), :] for k in range(3)] for i in indices
        ]
        slope = [(nodes[1][k] - nodes[0][k]) * 0.125 for k in range(3)]
        for c in range(cells):
            next_slope = [(nodes[c + 2][k] - nodes[c + 1][k]) * 0.125 for k in range(3)]
            block = ref_in[pl.ds(x0 + c * 8, 8)]
            wide = [before if c == 0 else ref_in[x0 + c * 8 - 1].astype(F32)]
            wide += [block[s].astype(F32) for s in range(8)]
            wide += [after if c == cells - 1 else ref_in[x0 + c * 8 + 8].astype(F32)]
            for s in range(8):
                if s == 0:
                    value = [nodes[c + 1][k] - 3.5 * slope[k] for k in range(3)]
                elif s == 4:
                    slope = next_slope
                    value = [nodes[c + 1][k] + 0.5 * slope[k] for k in range(3)]
                else:
                    value = [value[k] + slope[k] for k in range(3)]
                x = x0 + c * 8 + s
                total = def_in[x].astype(F32) - wide[s + 1]
                total = total - (wide[s + 2] - wide[s]) * value[0]
                line = c * 8 + s
                y_edge = jnp.where(row == 0, -y_lows[line : line + 1], 0.0)
                y_edge = jnp.where(row == 15, y_highs[line : line + 1], y_edge)
                total = total - (slopes[0, x] + y_edge) * value[1]
                total = total - slopes[1, x] * value[2]
                out_buf[x] = total.astype(BF16)
        send(step).start()
        return 0

    lax.fori_loop(0, steps, body, 0)
    for step in range(steps):
        send(step).wait()


def solution(mesh):
    gx, gy, gz = (mesh.shape[a] for a in ("gx", "gy", "gz"))

    def on_device(ref_image, def_image, displacement):
        sizex, sizey, sizez = ref_image.shape
        rows = sizex // 8
        weights, table = solve_tables(gx, rows)
        chunk = 64
        disp = jnp.transpose(displacement, (0, 2, 3, 1))
        coarse_shape = (2, rows, 128)
        z_rows = 3 * rows + 32
        y_rows = 3 * rows + sizex
        params = pltpu.CompilerParams(vmem_limit_bytes=VMEM_BYTES)
        first_params = pltpu.CompilerParams(vmem_limit_bytes=FIRST_VMEM_BYTES)
        coarse, up, down, y_high, y_low = pl.pallas_call(
            lambda *refs: bin_kernel(chunk, *refs),
            name="bin_and_pack",
            in_specs=[HBM] * 3,
            out_specs=[VMEM] * 5,
            out_shape=[
                jax.ShapeDtypeStruct(coarse_shape, F32),
                jax.ShapeDtypeStruct((z_rows, 128), BF16),
                jax.ShapeDtypeStruct((z_rows, 128), BF16),
                jax.ShapeDtypeStruct((sizex, 128), BF16),
                jax.ShapeDtypeStruct((sizex, 128), BF16),
            ],
            scratch_shapes=[
                pltpu.VMEM(ref_image.shape, BF16),
                pltpu.VMEM(def_image.shape, BF16),
                pltpu.VMEM(disp.shape, F32),
                pltpu.VMEM((2, 2, rows, 128), F32),
                pltpu.VMEM((2, 32, 128), F32),
                pltpu.SemaphoreType.DMA((2, sizex // chunk)),
                pltpu.SemaphoreType.DMA,
            ],
            compiler_params=first_params,
        )(ref_image, def_image, disp)
        z_low = lax.ppermute(up, "gz", [(i, (i + 1) % gz) for i in range(gz)])
        z_high = lax.ppermute(down, "gz", [((i + 1) % gz, i) for i in range(gz)])
        coarse, down, up = pl.pallas_call(
            lambda *refs: z_kernel(gz, *refs),
            name="extend_along_z",
            in_specs=[VMEM] * 5,
            out_specs=[VMEM] * 3,
            out_shape=[
                jax.ShapeDtypeStruct(coarse_shape, F32),
                jax.ShapeDtypeStruct((y_rows, 128), BF16),
                jax.ShapeDtypeStruct((y_rows, 128), BF16),
            ],
            compiler_params=params,
        )(coarse, z_low, z_high, y_high, y_low)
        above = lax.ppermute(down, "gy", [(i + 1, i) for i in range(gy - 1)])
        below = lax.ppermute(up, "gy", [(i, i + 1) for i in range(gy - 1)])
        slopes_shape = (2,) + ref_image.shape
        chunks = rows // 4
        slopes = pl.pallas_call(
            gradient_kernel,
            name="gradients",
            in_specs=[VMEM] * 3,
            out_specs=VMEM,
            out_shape=jax.ShapeDtypeStruct(slopes_shape, F32),
            scratch_shapes=[pltpu.VMEM((2, rows, 128), F32)],
            compiler_params=params,
        )(z_low, z_high, ref_image)
        slabs, rhs, disp = pl.pallas_call(
            rhs_kernel,
            name="right_hand_sides",
            in_specs=[VMEM] * 5 + [pl.BlockSpec(memory_space=pl.ANY)],
            out_specs=[VMEM] * 3,
            out_shape=[
                jax.ShapeDtypeStruct((gx, SLAB, 128), BF16),
                jax.ShapeDtypeStruct((3, rows, 128), F32),
                jax.ShapeDtypeStruct((3, rows, 128), F32),
            ],
            compiler_params=params,
        )(coarse, above, below, ref_image, jnp.asarray(weights), slopes)
        slabs = lax.all_to_all(slabs, "gx", 0, 0, tiled=True)
        new, residual = pl.pallas_call(
            fine_kernel,
            name="solve_and_residual",
            in_specs=[VMEM] * 10,
            out_specs=[VMEM, HBM],
            out_shape=[
                jax.ShapeDtypeStruct((3, 2, 16, rows), F32),
                jax.ShapeDtypeStruct(ref_image.shape, BF16),
            ],
            scratch_shapes=[
                pltpu.VMEM((gx, 32, 128), F32),
                pltpu.VMEM((16 * 3 * EXT, 128), F32),
                pltpu.VMEM(ref_image.shape, BF16),
                pltpu.SemaphoreType.DMA((chunks,)),
            ],
            compiler_params=params,
        )(
            slabs, rhs, disp, jnp.asarray(table), jnp.asarray(prolong_table(sizey, sizez)),
            slopes, above, below, ref_image, def_image,
        )
        return jnp.transpose(new, (0, 3, 1, 2)), residual

    return jax.shard_map(
        on_device,
        mesh=mesh,
        in_specs=(P("gx", "gy", "gz"), P("gx", "gy", "gz"), P(None, "gx", "gy", "gz")),
        out_specs=(P(None, "gx", "gy", "gz"), P("gx", "gy", "gz")),
        check_vma=False,
    )
```
